256 devices in a mesh: blk: 16 (over z_hi, y), shard: 16 (over x, z_lo, core).
Axes of the slice: x: 4, y: 4, z: 8 (z_hi: 4, z_lo: 2; z = z_hi * 2 + z_lo), core: 2. Of those that a mesh axis runs over, the one named last changes fastest.
Arguments:
- picture_vectors: bfloat16 [65536, 1152], P(('blk', 'shard')), may hold values from -0.18 to 0.18
- sentence_vectors: bfloat16 [524288, 1152], P(('blk', 'shard')), may hold values from -0.18 to 0.18
- slot_picture_number: int32 [524288], P(('blk', 'shard')), may hold values from 0 to 256, as said below
- score_multiplier: float32 [], replicated, may hold values from 5 to 10
- score_offset: float32 [], replicated, may hold values from -3 to -1
Outputs:
- loss_rows: float32 [65536], P(('blk', 'shard'))
- grad_images: bfloat16 [65536, 1152], P(('blk', 'shard'))
- grad_captions: bfloat16 [524288, 1152], P(('blk', 'shard'))
The draws below stay inside these ranges and needn't reach their ends.
Inputs may be any that keep to these rules, and one draw needn't show every extreme that they name: `slot_picture_number`: in each block of 128 slots of a text device for one owner, live slots come first, in nondecreasing image order, and the rest hold 256. Every image is named by 1 to 5 of its owner's slots. Each owner has one block of 128 live slots whenever 128 <= 256.
All inputs are finite; a program needn't handle non-finite values.
Results may differ from the reference program's by a relative error of at most 0.017.
Values may be sent and summed in bfloat16 or wider, within the bound.
A program may use at most 128 MiB of HBM per device.

```python
import jax
import jax.numpy as jnp
from jax import lax

D = 1152
IMG_DEV = 256
CAPS_MAX = 5
SLOT = 128
NI = 65536
NCAP = 524288
N_BLK = 16
N_SHARD = 16


def caption_tables(seed_key):
    count_key, busy_key = jax.random.split(seed_key)
    owners = N_BLK * N_SHARD
    counts = jax.random.randint(count_key, (owners, IMG_DEV), 1, CAPS_MAX + 1).astype(jnp.int32)
    busy_source = jax.random.randint(busy_key, (owners,), 0, N_SHARD).astype(jnp.int32)
    count_ends = jnp.cumsum(counts, axis=1).astype(jnp.int32)
    caption_order = jnp.arange(CAPS_MAX * IMG_DEV, dtype=jnp.int32)
    image_of = jax.vmap(lambda count_row: jnp.searchsorted(count_row, caption_order, side='right'))(count_ends).astype(jnp.int32)
    is_live = caption_order[None, :] < count_ends[:, -1:]
    leading = caption_order[None, :] < SLOT
    later_index = jnp.maximum(caption_order - SLOT, 0)[None, :]
    other_index = later_index % (N_SHARD - 1)
    text_source = jnp.where(leading, busy_source[:, None], other_index + (other_index >= busy_source[:, None]).astype(jnp.int32))
    slot_place = jnp.where(leading, caption_order[None, :], later_index // (N_SHARD - 1))
    owner_index = jnp.arange(owners, dtype=jnp.int32)[:, None]
    group_index = owner_index // N_SHARD
    dest_index = owner_index % N_SHARD
    flat_index = ((group_index * N_SHARD + text_source) * N_SHARD + dest_index) * SLOT + slot_place
    flat_index = jnp.where(is_live, flat_index, NCAP).astype(jnp.int32)
    values = jnp.where(is_live, image_of, IMG_DEV).astype(jnp.int32)
    slot_table = jnp.full((NCAP + 1,), IMG_DEV, jnp.int32).at[flat_index.reshape(-1)].set(values.reshape(-1))
    return (counts.reshape(NI), slot_table[:NCAP])


def cluster_basis(seed_key):
    basis_key = jax.random.fold_in(seed_key, 101)
    family_key, member_key, pick_key = jax.random.split(basis_key, 3)
    families = jax.random.normal(family_key, (8, D), jnp.float32)
    members = jax.random.normal(member_key, (64, D), jnp.float32)
    family_of = jnp.arange(64, dtype=jnp.int32) // 8
    centers = 0.7 * families[family_of] + 0.71 * members
    image_cluster = jax.random.randint(pick_key, (NI,), 0, 64).astype(jnp.int32)
    return (centers, image_cluster)


def mixed_rows(key, centers_taken, row_count):
    weight_key, noise_key = jax.random.split(key, 2)
    mixing = jax.random.uniform(weight_key, (row_count, 1), jnp.float32, 0.3, 0.95)
    noise = jax.random.normal(noise_key, (row_count, D), jnp.float32)
    row_scale = jnp.ones((row_count, 1), jnp.float32)
    rows = mixing * centers_taken + jnp.sqrt(1.0 - mixing * mixing) * noise
    return jnp.clip(0.03 * row_scale * rows, -0.1797, 0.1797).astype(jnp.bfloat16)


def draw_picture_vectors(key, part):
    centers, image_cluster = cluster_basis(key)
    key = jax.random.fold_in(key, 7)
    return mixed_rows(key, centers[image_cluster], NI)


def draw_sentence_vectors(key, part):
    centers, image_cluster = cluster_basis(key)
    slot_table = caption_tables(key)[1]
    key = jax.random.fold_in(key, 11)
    slot_index = jnp.arange(NCAP, dtype=jnp.int32)
    group_index = slot_index // (N_SHARD * N_SHARD * SLOT)
    dest_index = slot_index // SLOT % N_SHARD
    image_global = (group_index * N_SHARD + dest_index) * IMG_DEV + jnp.minimum(slot_table, IMG_DEV - 1)
    slot_cluster = image_cluster[image_global]
    return mixed_rows(key, centers[slot_cluster], NCAP)


def draw_slot_picture_number(key, part):
    shared = caption_tables(key)
    return shared[1]


def setup_inputs(seed: int = 0) -> dict:
    seeds = jax.random.split(jax.random.key(seed), 6)
    return {
        "picture_vectors": draw_picture_vectors(jax.random.fold_in(seeds[5], 71), 0),
        "sentence_vectors": draw_sentence_vectors(jax.random.fold_in(seeds[5], 71), 0),
        "slot_picture_number": draw_slot_picture_number(jax.random.fold_in(seeds[5], 71), 0),
        "score_multiplier": jnp.clip(jax.random.uniform(seeds[3], (), jnp.float32, 5.0, 10.0), 5.0, 10.0),
        "score_offset": jnp.clip(jax.random.uniform(seeds[4], (), jnp.float32, -3.0, -1.0), -3.0, -1.0),
    }


EPS = 1e-06

def reference(picture_vectors, sentence_vectors, slot_picture_number, score_multiplier, score_offset):
    feature_width = picture_vectors.shape[1]
    column = IMG_DEV * N_BLK
    per_owner = N_SHARD * SLOT
    caption_grid = sentence_vectors.reshape(N_BLK, N_SHARD, N_SHARD, SLOT, feature_width)
    slot_ids = slot_picture_number.reshape(N_BLK, N_SHARD, N_SHARD, SLOT)
    targets = jnp.arange(IMG_DEV, dtype=jnp.int32)

    def pool_owner(owner_index):
        group_index = owner_index // N_SHARD
        dest_index = owner_index % N_SHARD
        row_block = caption_grid[group_index][:, dest_index].reshape(per_owner, feature_width)
        owner_ids = slot_ids[group_index][:, dest_index].reshape(per_owner)
        onehot = (owner_ids[None, :] == targets[:, None]).astype(jnp.bfloat16)
        return jnp.dot(onehot, row_block, preferred_element_type=jnp.float32)
    summed = lax.map(pool_owner, jnp.arange(N_BLK * N_SHARD, dtype=jnp.int32))
    pooled = summed.reshape(N_BLK, N_SHARD, IMG_DEV, feature_width)
    text_norm = jnp.sqrt(lax.optimization_barrier(jnp.sum(pooled * pooled, axis=-1, keepdims=True)) + EPS)
    text_unit = pooled / text_norm
    text_half = text_unit.astype(jnp.bfloat16)
    image_rows = picture_vectors.reshape(N_BLK, N_SHARD, IMG_DEV, feature_width).astype(jnp.float32)
    image_norm = jnp.sqrt(lax.optimization_barrier(jnp.sum(image_rows * image_rows, axis=-1, keepdims=True)) + EPS)
    image_unit = image_rows / image_norm
    picture_vector_share = image_unit.astype(jnp.bfloat16)
    column_ids = jnp.arange(column, dtype=jnp.int32)

    def column_pass(shard_index):
        image_column = picture_vector_share[:, shard_index]
        sentence_entry_range = text_half[:, shard_index].reshape(column, feature_width)

        def block_pass(text_grad, block_index):
            picture_group_matrix = image_column[block_index]
            match_scores = score_multiplier * jnp.dot(picture_group_matrix, sentence_entry_range.T, preferred_element_type=jnp.float32) + score_offset
            row_ids = block_index * IMG_DEV + jnp.arange(IMG_DEV, dtype=jnp.int32)
            label_sign_table = jnp.where(row_ids[:, None] == column_ids[None, :], 1.0, -1.0).astype(jnp.float32)
            signed_logits = label_sign_table * match_scores
            loss_part = lax.optimization_barrier(jnp.sum(-jax.nn.log_sigmoid(signed_logits), axis=1)) / column
            match_derivatives = (-label_sign_table * jax.nn.sigmoid(-signed_logits)).astype(jnp.bfloat16)
            picture_derivative = score_multiplier * jnp.dot(match_derivatives, sentence_entry_range, preferred_element_type=jnp.float32)
            sentence_incomplete_summand = (score_multiplier * jnp.dot(match_derivatives.T, picture_group_matrix, preferred_element_type=jnp.float32)).astype(jnp.bfloat16)
            return (text_grad + sentence_incomplete_summand.astype(jnp.float32), (loss_part, picture_derivative))
        start_grad = jnp.zeros((column, feature_width), jnp.float32)
        text_grad, (loss_part, picture_derivative) = lax.scan(block_pass, start_grad, jnp.arange(N_BLK, dtype=jnp.int32))
        return (loss_part, picture_derivative, text_grad.reshape(N_BLK, IMG_DEV, feature_width))
    loss_part, picture_derivative, text_grad = lax.map(column_pass, jnp.arange(N_SHARD, dtype=jnp.int32))
    loss_rows = jnp.transpose(loss_part, (1, 0, 2)).reshape(NI)
    picture_derivative = jnp.transpose(picture_derivative, (1, 0, 2, 3))
    text_grad = jnp.transpose(text_grad, (1, 0, 2, 3))
    grad_images = ((picture_derivative - image_unit * lax.optimization_barrier(jnp.sum(image_unit * picture_derivative, axis=-1, keepdims=True))) / image_norm).astype(jnp.bfloat16)
    pool_grad = (text_grad - text_unit * lax.optimization_barrier(jnp.sum(text_unit * text_grad, axis=-1, keepdims=True))) / text_norm
    scaled = pool_grad.astype(jnp.bfloat16)
    padded = jnp.concatenate([scaled, jnp.zeros((N_BLK, N_SHARD, 1, feature_width), jnp.bfloat16)], axis=2)
    padded = padded.reshape(N_BLK * N_SHARD * (IMG_DEV + 1), feature_width)
    slot_index = jnp.arange(NCAP, dtype=jnp.int32)
    group_index = slot_index // (N_SHARD * N_SHARD * SLOT)
    dest_index = slot_index // SLOT % N_SHARD
    lookup = (group_index * N_SHARD + dest_index) * (IMG_DEV + 1) + slot_picture_number.astype(jnp.int32)
    grad_captions = jnp.take(padded, lookup, axis=0)
    return (loss_rows, grad_images.reshape(NI, feature_width), grad_captions)
```

```python
import jax
import jax.numpy as jnp
from jax import lax
from jax.experimental import pallas as pl
from jax.experimental.pallas import tpu as pltpu
from jax.sharding import PartitionSpec as P

EPS = 1e-06
D = 1152
ROWS = 256
SLOT = 128
NB = 16
TOTAL = NB * ROWS
F32 = jnp.float32
BF16 = jnp.bfloat16
CHUNK = 384
CHUNKS = D // CHUNK
N_COPY = 72


def pair_terms(scores, diagonal):
    u = jnp.where(diagonal, -scores, scores)
    e = jnp.exp(-jnp.abs(u))
    r = 1.0 / (1.0 + e)
    sig = jnp.where(u >= 0, r, e * r)
    return u, e, jnp.where(diagonal, -sig, sig)


def kernel(
    mult_ref,
    off_ref,
    ids_ref,
    img_ref,
    cap_ref,
    loss_ref,
    gimg_ref,
    gcap_ref,
    xr,
    idr,
    imgs,
    txts,
    psend,
    prec,
    hot,
    hot_t,
    g2,
    g1,
    tsum,
    tgrad,
    igrad,
    sc,
    gsend,
    grecv,
    lsend,
    lrecv,
    lown,
    send_sem,
    recv_sem,
    local_sem,
):
    g = lax.axis_index("blk")
    h = lax.axis_index("shard")
    zh, y = lax.div(g, 4), lax.rem(g, 4)
    x, w = lax.div(h, 4), lax.rem(h, 4)

    def ring(value, step):
        return lax.rem(value + step, 4)

    def at_x(step):
        return (g, ring(x, step) * 4 + w)

    def at_w(step):
        return (g, x * 4 + ring(w, step))

    def at_z(step):
        return (ring(zh, step) * 4 + y, h)

    def at_y(step):
        return (zh * 4 + ring(y, step), h)

    made = []
    local = []

    def send(src, dst, device):
        k = len(made)
        copy = pltpu.make_async_remote_copy(
            src_ref=src,
            dst_ref=dst,
            send_sem=send_sem.at[k],
            recv_sem=recv_sem.at[k],
            device_id=device,
            device_id_type=pl.DeviceIdType.MESH,
        )
        copy.start()
        made.append(copy)
        return copy

    def move(src, dst):
        copy = pltpu.make_async_copy(src, dst, local_sem.at[len(local)])
        copy.start()
        local.append(copy)
        return copy

    def rows(block, first=0, count=ROWS):
        return pl.ds(pl.multiple_of(block * ROWS + first, 128), count)

    def cols(j):
        return slice(j * CHUNK, (j + 1) * CHUNK)

    barrier = pltpu.get_barrier_semaphore()
    partners = [at_x(s) for s in (1, 2, 3)] + [at_w(s) for s in (1, 2, 3)]
    partners += [at_z(s) for s in (1, 3)] + [at_y(s) for s in (1, 2, 3)]
    for device in partners:
        pl.semaphore_signal(barrier, inc=1, device_id=device, device_id_type=pl.DeviceIdType.MESH)
    pl.semaphore_wait(barrier, len(partners))

    id_copies = [send(ids_ref.at[ring(x, s)], idr.at[x], at_x(s)) for s in (2, 1, 3)]
    id_own = move(ids_ref.at[x], idr.at[x])
    x_copies, x_own = [], []
    for j in range(CHUNKS):
        x_copies.append(
            [
                send(
                    cap_ref.at[pl.ds(pl.multiple_of(ring(x, s) * 512, 512), 512), cols(j)],
                    xr.at[x, :, cols(j)],
                    at_x(s),
                )
                for s in (2, 1, 3)
            ]
        )
        x_own.append(
            move(
                cap_ref.at[pl.ds(pl.multiple_of(x * 512, 512), 512), cols(j)], xr.at[x, :, cols(j)]
            )
        )

    pics = img_ref[...].astype(F32)
    pic_norm = jnp.sqrt(jnp.sum(pics * pics, axis=-1, keepdims=True) + EPS)
    imgs[rows(g), :] = (pics / pic_norm).astype(BF16)

    def start_y(step):
        block = ring(zh, step) * 4 + y
        piece = imgs.at[rows(block)]
        return [send(piece, piece, at_y(1)), send(piece, piece, at_y(3))]

    def forward_y(step, copies):
        up, down = copies
        up.wait_recv()
        piece = imgs.at[rows(ring(zh, step) * 4 + ring(y, 3), 0, 128)]
        first = send(piece, piece, at_y(1))
        down.wait_recv()
        piece = imgs.at[rows(ring(zh, step) * 4 + ring(y, 1), 128, 128)]
        return [first, send(piece, piece, at_y(3))]

    piece = imgs.at[rows(g)]
    z_copies = [send(piece, piece, at_z(1)), send(piece, piece, at_z(3))]
    y_first = {0: start_y(0)}
    y_halves = {0: forward_y(0, y_first[0])}

    z_copies[0].wait_recv()
    piece = imgs.at[rows(ring(zh, 3) * 4 + y, 0, 128)]
    z_halves = [send(piece, piece, at_z(1))]
    y_first[3] = start_y(3)
    z_copies[1].wait_recv()
    piece = imgs.at[rows(ring(zh, 1) * 4 + y, 128, 128)]
    z_halves.append(send(piece, piece, at_z(3)))
    y_first[1] = start_y(1)

    id_own.wait()
    for copy in id_copies:
        copy.wait_recv()
    image_rows = lax.broadcasted_iota(jnp.int32, (ROWS, SLOT), 0)
    for o in range(4):
        for s in range(4):
            table = (idr[s, o : o + 1, :] == image_rows).astype(F32)
            hot[o, :, s * SLOT : (s + 1) * SLOT] = table.astype(BF16)
            hot_t[o, s * SLOT : (s + 1) * SLOT, :] = table.T.astype(BF16)

    def pool(j):
        x_own[j].wait()
        for copy in x_copies[j]:
            copy.wait_recv()
        for o in range(4):
            stack = jnp.concatenate(
                [xr[s, o * SLOT : (o + 1) * SLOT, cols(j)] for s in range(4)], axis=0
            )
            psend[o, :, cols(j)] = jnp.dot(
                hot[o], stack, preferred_element_type=F32
            ).astype(BF16)
        return [
            send(psend.at[ring(w, s), :, cols(j)], prec.at[w, :, cols(j)], at_w(s))
            for s in (1, 2, 3)
        ]

    p_copies = [pool(0)]
    for copy in z_halves:
        copy.wait_recv()
    y_first[2] = start_y(2)
    y_halves[3] = forward_y(3, y_first[3])
    p_copies.append(pool(1))
    y_halves[1] = forward_y(1, y_first[1])
    p_copies.append(pool(2))
    y_halves[2] = forward_y(2, y_first[2])

    square = jnp.zeros((ROWS, 1), F32)
    for j in range(CHUNKS):
        for copy in p_copies[j]:
            copy.wait_recv()
        total = psend[w, :, cols(j)].astype(F32)
        for s in (1, 2, 3):
            total += prec[ring(w, s), :, cols(j)].astype(F32)
        tsum[:, cols(j)] = total
        square += jnp.sum(total * total, axis=-1, keepdims=True)
    text_norm = jnp.sqrt(square + EPS)
    unit = tsum[...] / text_norm
    tsum[...] = unit
    txts[rows(zh), :] = unit.astype(BF16)
    piece = txts.at[rows(zh)]
    t_copies = [send(piece, piece, at_z(1)), send(piece, piece, at_z(3))]

    mult, off = mult_ref[0], off_ref[0]
    gap = lax.broadcasted_iota(jnp.int32, (ROWS, ROWS), 0) - lax.broadcasted_iota(
        jnp.int32, (ROWS, ROWS), 1
    )
    nt = (((1,), (1,)), ((), ()))

    for step in (0, 3, 1, 2):
        for copy in y_halves[step]:
            copy.wait_recv()

        def text_block(k, carry, step=step):
            block = ring(zh, step) * 4 + k
            scores = lax.dot_general(
                txts[rows(zh), :], imgs[rows(block), :], nt, preferred_element_type=F32
            )
            diagonal = gap == jnp.where(block == g, 0, 2 * ROWS)
            terms = pair_terms(mult * scores + off, diagonal)
            g2[:, rows(block)] = terms[2].astype(BF16)
            return carry

        lax.fori_loop(0, 4, text_block, 0)

    for j in range(CHUNKS):
        tgrad[:, cols(j)] = mult * jnp.dot(
            g2[...], imgs[:, cols(j)], preferred_element_type=F32
        )

    t_copies[0].wait_recv()
    piece = txts.at[rows(ring(zh, 3), 0, 128)]
    t_halves = [send(piece, piece, at_z(1))]
    t_copies[1].wait_recv()
    piece = txts.at[rows(ring(zh, 1), 128, 128)]
    t_halves.append(send(piece, piece, at_z(3)))

    along = jnp.sum(tsum[...] * tgrad[...], axis=-1, keepdims=True)
    s_copies = []
    for j in range(CHUNKS):
        sc[w, :, cols(j)] = (
            (tgrad[:, cols(j)] - tsum[:, cols(j)] * along) / text_norm
        ).astype(BF16)
        s_copies.append(
            [send(sc.at[w, :, cols(j)], sc.at[w, :, cols(j)], at_w(s)) for s in (1, 2, 3)]
        )

    out_copies, out_own = [], []
    for j in range(CHUNKS):
        for copy in s_copies[j]:
            copy.wait_recv()
        for s in (2, 1, 3, 0):
            for o in range(4):
                xr[ring(x, s), o * SLOT : (o + 1) * SLOT, cols(j)] = jnp.dot(
                    hot_t[o, pl.ds(pl.multiple_of(ring(x, s) * SLOT, SLOT), SLOT), :],
                    sc[o, :, cols(j)],
                    preferred_element_type=F32,
                ).astype(BF16)
            src = xr.at[ring(x, s), :, cols(j)]
            dst = gcap_ref.at[pl.ds(pl.multiple_of(x * 512, 512), 512), cols(j)]
            if s:
                out_copies.append(send(src, dst, at_x(s)))
            else:
                out_own.append(move(src, dst))

    for copy in t_halves:
        copy.wait_recv()
    i_copies = []
    for step in (2, 1, 3, 0):
        block = zh * 4 + ring(y, step)
        loss_part = jnp.zeros((ROWS, 128), F32)
        for k in range(4):
            scores = lax.dot_general(
                imgs[rows(block), :],
                txts[k * ROWS : (k + 1) * ROWS, :],
                nt,
                preferred_element_type=F32,
            )
            if step:
                diagonal = jnp.zeros((ROWS, ROWS), jnp.bool_)
            else:
                diagonal = gap == jnp.where(zh == k, 0, 2 * ROWS)
            u, e, grad = pair_terms(mult * scores + off, diagonal)
            losses = jnp.maximum(u, 0.0) + jnp.log1p(e)
            loss_part += losses[:, :128] + losses[:, 128:]
            g1[:, k * ROWS : (k + 1) * ROWS] = grad.astype(BF16)
        part = mult * jnp.dot(g1[...], txts[...], preferred_element_type=F32)
        if step:
            gsend[step - 1] = part.astype(BF16)
            lsend[step - 1] = loss_part
            i_copies.append(send(gsend.at[step - 1], grecv.at[step - 1], at_y(step)))
            i_copies.append(send(lsend.at[step - 1], lrecv.at[step - 1], at_y(step)))
        else:
            igrad[...] = part
            lown[...] = loss_part
    for copy in i_copies:
        copy.wait_recv()

    losses = lown[...] + lrecv[0] + lrecv[1] + lrecv[2]
    loss_ref[...] = jnp.sum(losses.T, axis=0, keepdims=True) / TOTAL
    total = igrad[...]
    for s in range(3):
        total += grecv[s].astype(F32)
    pics = img_ref[...].astype(F32)
    pic_norm = jnp.sqrt(jnp.sum(pics * pics, axis=-1, keepdims=True) + EPS)
    unit = pics / pic_norm
    along = jnp.sum(unit * total, axis=-1, keepdims=True)
    gimg_ref[...] = ((total - unit * along) / pic_norm).astype(BF16)

    for copy in out_copies:
        copy.wait_recv()
    for copy in out_own:
        copy.wait()
    for copy in made:
        copy.wait_send()


def body(picture_vectors, sentence_vectors, slot_picture_number, score_multiplier, score_offset):
    vmem = pl.BlockSpec(memory_space=pltpu.VMEM)
    smem = pl.BlockSpec(memory_space=pltpu.SMEM)
    anywhere = pl.BlockSpec(memory_space=pl.ANY)
    loss, grad_images, grad_captions = pl.pallas_call(
        kernel,
        out_shape=(
            jax.ShapeDtypeStruct((1, ROWS), F32),
            jax.ShapeDtypeStruct((ROWS, D), BF16),
            jax.ShapeDtypeStruct((16 * SLOT, D), BF16),
        ),
        in_specs=[smem, smem, vmem, vmem, anywhere],
        out_specs=(vmem, vmem, anywhere),
        scratch_shapes=[
            pltpu.VMEM((4, 512, D), BF16),
            pltpu.VMEM((4, 4, SLOT), jnp.int32),
            pltpu.VMEM((TOTAL, D), BF16),
            pltpu.VMEM((4 * ROWS, D), BF16),
            pltpu.VMEM((4, ROWS, D), BF16),
            pltpu.VMEM((4, ROWS, D), BF16),
            pltpu.VMEM((4, ROWS, 4 * SLOT), BF16),
            pltpu.VMEM((4, 4 * SLOT, ROWS), BF16),
            pltpu.VMEM((ROWS, TOTAL), BF16),
            pltpu.VMEM((ROWS, 4 * ROWS), BF16),
            pltpu.VMEM((ROWS, D), F32),
            pltpu.VMEM((ROWS, D), F32),
            pltpu.VMEM((ROWS, D), F32),
            pltpu.VMEM((4, ROWS, D), BF16),
            pltpu.VMEM((3, ROWS, D), BF16),
            pltpu.VMEM((3, ROWS, D), BF16),
            pltpu.VMEM((3, ROWS, 128), F32),
            pltpu.VMEM((3, ROWS, 128), F32),
            pltpu.VMEM((ROWS, 128), F32),
            pltpu.SemaphoreType.DMA((N_COPY,)),
            pltpu.SemaphoreType.DMA((N_COPY,)),
            pltpu.SemaphoreType.DMA((8,)),
        ],
        compiler_params=pltpu.CompilerParams(
            collective_id=0, has_side_effects=True, vmem_limit_bytes=56 * 1024 * 1024
        ),
        cost_estimate=pl.CostEstimate(
            flops=13_000_000_000, bytes_accessed=12_000_000, transcendentals=4_000_000
        ),
        name="pooled_sigmoid_loss",
    )(
        score_multiplier.reshape(1),
        score_offset.reshape(1),
        slot_picture_number.reshape(4, 4, SLOT),
        picture_vectors,
        sentence_vectors,
    )
    return loss.reshape(ROWS), grad_images, grad_captions


def solution(mesh):
    return jax.shard_map(
        body,
        mesh=mesh,
        in_specs=(
            P(("blk", "shard"), None),
            P(("blk", "shard"), None),
            P(("blk", "shard")),
            P(),
            P(),
        ),
        out_specs=(P(("blk", "shard")), P(("blk", "shard"), None), P(("blk", "shard"), None)),
        check_vma=False,
    )
```

```python
import jax
import jax.numpy as jnp
from jax import lax
from jax.experimental import pallas as pl
from jax.experimental.pallas import tpu as pltpu
from jax.sharding import PartitionSpec as P

EPS = 1e-06
D = 1152
ROWS = 256
SLOT = 128
NB = 16
TOTAL = NB * ROWS
F32 = jnp.float32
BF16 = jnp.bfloat16
WIDTHS_IN = (384, 384, 256, 128)
WIDTHS_OUT = (128, 256, 384, 384)
N_COPY = 88


def spans(widths):
    starts = [sum(widths[:i]) for i in range(len(widths))]
    return [slice(s, s + n) for s, n in zip(starts, widths)]


IN, OUT = spans(WIDTHS_IN), spans(WIDTHS_OUT)


class Copy:
    def __init__(self, copy, when):
        self.copy, self.when = copy, when

    def act(self, step):
        if self.when is None:
            step()
        else:
            pl.when(self.when)(step)

    def wait_recv(self):
        self.act(self.copy.wait_recv)

    def wait_send(self):
        self.act(self.copy.wait_send)


def pair_gradient(scores, diagonal):
    u = jnp.where(diagonal, -scores, scores)
    sig = 1.0 / (1.0 + jnp.exp(-u))
    return jnp.where(diagonal, -sig, sig)


def pair_loss(scores, diagonal):
    u = jnp.where(diagonal, -scores, scores)
    return jnp.maximum(u, 0.0) + jnp.log1p(jnp.exp(-jnp.abs(u)))


def kernel(
    mult_ref,
    off_ref,
    ids_ref,
    img_ref,
    cap_ref,
    loss_ref,
    gimg_ref,
    gcap_ref,
    xr,
    idr,
    imgs,
    txts,
    psib,
    prsib,
    psend,
    prec,
    hot,
    hot_t,
    g2,
    g1,
    tsum,
    tgrad,
    tswap,
    sc,
    gsend,
    grecv,
    lsend,
    lrecv,
    send_sem,
    recv_sem,
    local_sem,
):
    g = lax.axis_index("blk")
    h = lax.axis_index("shard")
    zh, y = lax.div(g, 4), lax.rem(g, 4)
    x, w = lax.div(h, 4), lax.rem(h, 4)
    za, zb = lax.div(zh, 2), lax.rem(zh, 2)
    zl, b = lax.div(w, 2), lax.rem(w, 2)
    on = zb == b
    off = zb != b

    def ring(value, step):
        return lax.rem(value + step, 4)

    def at_x(step):
        return (g, ring(x, step) * 4 + w)

    def at_y(step):
        return (zh * 4 + ring(y, step), h)

    core = (g, x * 4 + zl * 2 + 1 - b)
    flipped = x * 4 + zl * 2 + 1 - b
    up = (jnp.where(on, ring(zh, 2), ring(zh, 1)) * 4 + y, jnp.where(on, h, flipped))
    down = (ring(zh, 3) * 4 + y, flipped)

    def partner(step):
        z = jnp.where(on, zh, za * 2 + 1 - zb)
        c = jnp.where(on, b, 1 - b)
        return (z * 4 + y, x * 4 + (1 - zl if step else zl) * 2 + c)

    made = []
    local = []

    def send(src, dst, device, when=None, start=True):
        k = len(made)
        copy = pltpu.make_async_remote_copy(
            src_ref=src,
            dst_ref=dst,
            send_sem=send_sem.at[k],
            recv_sem=recv_sem.at[k],
            device_id=device,
            device_id_type=pl.DeviceIdType.MESH,
        )
        made.append(Copy(copy, when))
        if start:
            made[-1].act(copy.start)
        return made[-1]

    def move(src, dst):
        copy = pltpu.make_async_copy(src, dst, local_sem.at[len(local)])
        copy.start()
        local.append(copy)
        return copy

    def rows(block, first=0, count=ROWS):
        return pl.ds(pl.multiple_of(block * ROWS + first, 128), count)

    def piece(owner):
        return pl.ds(pl.multiple_of(owner * 512, 512), 512)

    barrier = pltpu.get_barrier_semaphore()

    def greet(device):
        pl.semaphore_signal(barrier, inc=1, device_id=device, device_id_type=pl.DeviceIdType.MESH)

    partners = [at_x(s) for s in (1, 2, 3)] + [at_y(s) for s in (1, 3)]
    partners += [core, up, partner(1)]
    for device in partners:
        greet(device)

    @pl.when(off)
    def _():
        for device in (down, partner(0)):
            greet(device)

    pl.semaphore_wait(barrier, len(partners) + jnp.where(on, 0, 2))

    id_copies = [send(ids_ref.at[ring(x, s)], idr.at[x], at_x(s)) for s in (2, 1, 3)]
    id_own = move(ids_ref.at[x], idr.at[x])
    x_copies, x_own = [], []
    for span in IN:
        x_copies.append(
            [
                send(cap_ref.at[piece(ring(x, s)), span], xr.at[x, :, span], at_x(s))
                for s in (2, 1, 3)
            ]
        )
        x_own.append(move(cap_ref.at[piece(x), span], xr.at[x, :, span]))

    pics = img_ref[...].astype(F32)
    pic_norm = jnp.sqrt(jnp.sum(pics * pics, axis=-1, keepdims=True) + EPS)
    imgs[rows(y), :] = (pics / pic_norm).astype(BF16)
    first = jnp.where(on, 0, 4)
    z_near = jnp.where(on, zh, ring(zh, 3))
    z_far = jnp.where(on, ring(zh, 2), ring(zh, 1))

    def round_y(buffer, slot, start=True):
        src = buffer.at[rows(slot(y))]
        return [send(src, src, at_y(s), start=start) for s in (1, 3)]

    def pass_y(buffer, slot, copies, step):
        copies[0 if step == 3 else 1].wait_recv()
        src = buffer.at[rows(slot(ring(y, step)), 0 if step == 3 else 128, 128)]
        return send(src, src, at_y(4 - step))

    def near_slot(k):
        return first + k

    def far_slot(k):
        return first + 4 + k

    def text_slot(k):
        return k * 2 + b

    src = imgs.at[rows(y)]
    up_copy = send(src, imgs.at[rows(4 + y)], up)
    down_copy = send(src, imgs.at[rows(8 + y)], down, when=off)
    near = round_y(imgs, near_slot, start=False)
    far = round_y(imgs, far_slot, start=False)

    @pl.when(on)
    def _():
        for copy in near:
            copy.copy.start()

    id_own.wait()
    for copy in id_copies:
        copy.wait_recv()
    image_rows = lax.broadcasted_iota(jnp.int32, (ROWS, SLOT), 0)
    for o in range(4):
        for s in range(4):
            table = (idr[s, o : o + 1, :] == image_rows).astype(F32)
            hot[o, :, s * SLOT : (s + 1) * SLOT] = table.astype(BF16)
            hot_t[o, s * SLOT : (s + 1) * SLOT, :] = table.T.astype(BF16)

    up_copy.wait_recv()

    @pl.when(on)
    def _():
        for copy in far:
            copy.copy.start()

    @pl.when(off)
    def _():
        for copy in near:
            copy.copy.start()

    down_copy.wait_recv()

    @pl.when(off)
    def _():
        for copy in far:
            copy.copy.start()

    p_copies = []

    def pooled(owner, span):
        block = pl.ds(pl.multiple_of(owner * SLOT, SLOT), SLOT)
        stack = jnp.concatenate([xr[s, block, span] for s in range(4)], axis=0)
        return jnp.dot(hot[owner], stack, preferred_element_type=F32)

    def pool(j):
        span = IN[j]
        x_own[j].wait()
        for copy in x_copies[j]:
            copy.wait_recv()
        for t in range(2):
            psib[t, :, span] = pooled(t * 2 + 1 - b, span).astype(BF16)
        sib = send(psib.at[:, :, span], prsib.at[:, :, span], core)
        sums = [pooled(t * 2 + b, span) for t in range(2)]
        sib.wait_recv()
        for t in range(2):
            psend[t, :, span] = (sums[t] + prsib[t, :, span].astype(F32)).astype(BF16)
        p_copies.append(
            [
                send(psend.at[1 - zl, :, span], prec.at[1, :, span], partner(1)),
                send(psend.at[zl, :, span], prec.at[0, :, span], partner(0), when=off),
            ]
        )

        @pl.when(on)
        def _():
            prec[0, :, span] = psend[zl, :, span]

    pool(0)
    halves = [pass_y(imgs, near_slot, near, step) for step in (3, 1)]
    pool(1)
    halves += [pass_y(imgs, far_slot, far, step) for step in (3, 1)]
    for j in range(2, len(IN)):
        pool(j)

    square = jnp.zeros((ROWS, 1), F32)
    for j, span in enumerate(IN):
        for copy in p_copies[j]:
            copy.wait_recv()
        total = prec[0, :, span].astype(F32) + prec[1, :, span].astype(F32)
        tsum[:, span] = total
        square += jnp.sum(total * total, axis=-1, keepdims=True)
    text_scale = lax.rsqrt(square + EPS)
    unit = tsum[...] * text_scale
    tsum[...] = unit
    txts[rows(text_slot(y)), :] = unit.astype(BF16)
    src = txts.at[rows(text_slot(y))]
    t_swaps = [send(src, src, core)]
    t_copies = round_y(txts, text_slot)

    mult, offset = mult_ref[0], off_ref[0]
    gap = lax.broadcasted_iota(jnp.int32, (ROWS, ROWS), 0) - lax.broadcasted_iota(
        jnp.int32, (ROWS, ROWS), 1
    )
    nt = (((1,), (1,)), ((), ()))
    def diagonal(same):
        return gap == jnp.where(same, 0, 2 * ROWS)

    for copy in halves:
        copy.wait_recv()
    t_swaps[0].wait_recv()
    both = pl.ds(pl.multiple_of(y * 2 * ROWS, 128), 2 * ROWS)
    for k in range(8):
        scores = lax.dot_general(
            txts[both, :], imgs[rows(first + k), :], nt, preferred_element_type=F32
        )
        image_z = z_far if k // 4 else z_near
        for t in range(2):
            same = (y == k % 4) & (image_z == za * 2 + t)
            block = slice(t * ROWS, (t + 1) * ROWS)
            grad = pair_gradient(mult * scores[block] + offset, diagonal(same))
            g2[block, k * ROWS : (k + 1) * ROWS] = grad.astype(BF16)
    parts = (slice(0, 512), slice(512, 1024), slice(1024, D))
    g_swaps = []
    for span in parts:
        tgrad[:, span] = mult * jnp.dot(
            g2[...],
            imgs[pl.ds(pl.multiple_of(first * ROWS, 128), 8 * ROWS), span],
            preferred_element_type=F32,
        )
        tswap[0, :, span] = tgrad[rows(1 - b), span].astype(BF16)
        g_swaps.append(send(tswap.at[0, :, span], tswap.at[1, :, span], core))

    along = jnp.zeros((ROWS, 1), F32)
    for copy, span in zip(g_swaps, parts):
        copy.wait_recv()
        total = tgrad[rows(b), span] + tswap[1, :, span].astype(F32)
        tgrad[rows(b), span] = total
        along += jnp.sum(tsum[:, span] * total, axis=-1, keepdims=True)
    s_copies = []
    for span in OUT:
        tswap[2, :, span] = (
            (tgrad[rows(b), span] - tsum[:, span] * along) * text_scale
        ).astype(BF16)
        src = tswap.at[2, :, span]
        s_copies.append(
            [
                send(src, sc.at[zb * 2 + zl, :, span], partner(1)),
                send(src, sc.at[zb * 2 + zl, :, span], partner(0), when=off),
            ]
        )

        @pl.when(on)
        def _():
            sc[zb * 2 + zl, :, span] = tswap[2, :, span]

    out_copies, out_own = [], []
    t_halves = []
    for j, span in enumerate(OUT):
        for copy in s_copies[j]:
            copy.wait_recv()
        src = sc.at[pl.ds(b * 2, 2), :, span]
        send(src, src, core).wait_recv()
        for s in (2, 1, 3, 0):
            for o in range(4):
                xr[ring(x, s), o * SLOT : (o + 1) * SLOT, span] = jnp.dot(
                    hot_t[o, pl.ds(pl.multiple_of(ring(x, s) * SLOT, SLOT), SLOT), :],
                    sc[o % 2 * 2 + o // 2, :, span],
                    preferred_element_type=F32,
                ).astype(BF16)
            src = xr.at[ring(x, s), :, span]
            dst = gcap_ref.at[piece(x), span]
            if s:
                out_copies.append(send(src, dst, at_x(s)))
            else:
                out_own.append(move(src, dst))
        if j == 1:
            t_halves = [pass_y(txts, text_slot, t_copies, step) for step in (3, 1)]
            for step in (3, 1):
                src = txts.at[rows(text_slot(ring(y, step)))]
                t_swaps.append(send(src, src, core))

    for copy in t_halves:
        copy.wait_recv()
    src = txts.at[rows(text_slot(ring(y, 2)))]
    t_swaps.append(send(src, src, core))
    for copy in t_swaps[1:]:
        copy.wait_recv()
    i_copies = []
    for far in (1, 0):
        image_z = z_far if far else z_near
        loss_part = jnp.zeros((ROWS, 128), F32)
        for k in range(8):
            scores = lax.dot_general(
                imgs[rows(first + far * 4 + y), :],
                txts[k * ROWS : (k + 1) * ROWS, :],
                nt,
                preferred_element_type=F32,
            )
            same = (y == k // 2) & (image_z == za * 2 + k % 2)
            scores = mult * scores + offset
            grad = pair_gradient(scores, diagonal(same))
            losses = pair_loss(scores, diagonal(same))
            loss_part += losses[:, :128] + losses[:, 128:]
            g1[:, k * ROWS : (k + 1) * ROWS] = grad.astype(BF16)
        gsend[far] = (
            mult * jnp.dot(g1[...], txts[...], preferred_element_type=F32)
        ).astype(BF16)
        lsend[far] = loss_part
        device, when = (up, None) if far else (down, off)
        i_copies.append(send(gsend.at[far], grecv.at[far], device, when))
        i_copies.append(send(lsend.at[far], lrecv.at[far], device, when))

    @pl.when(on)
    def _():
        grecv[0] = gsend[0]
        lrecv[0] = lsend[0]

    for copy in i_copies:
        copy.wait_recv()

    losses = lrecv[0] + lrecv[1]
    loss_ref[...] = jnp.sum(losses.T, axis=0, keepdims=True) / TOTAL
    total = grecv[0].astype(F32) + grecv[1].astype(F32)
    pics = img_ref[...].astype(F32)
    pic_norm = jnp.sqrt(jnp.sum(pics * pics, axis=-1, keepdims=True) + EPS)
    unit = pics / pic_norm
    along = jnp.sum(unit * total, axis=-1, keepdims=True)
    gimg_ref[...] = ((total - unit * along) / pic_norm).astype(BF16)

    for copy in out_copies:
        copy.wait_recv()
    for copy in out_own:
        copy.wait()
    for copy in made:
        copy.wait_send()


def hand_over(loss_ref, gimg_ref, gcap_ref, loss_out, gimg_out, gcap_out, held, in_sem, out_sem):
    pieces = [(gcap_ref, gcap_out, i * ROWS) for i in range(8)] + [(gimg_ref, gimg_out, 0)]
    ins, outs = [], []
    for i, (src, dst, row) in enumerate(pieces):
        part = pl.ds(row, ROWS)
        ins.append(pltpu.make_async_copy(src.at[part], held.at[i], in_sem.at[i]))
        outs.append(pltpu.make_async_copy(held.at[i], dst.at[part], out_sem.at[i]))
        ins[i].start()
    for i in range(len(pieces)):
        ins[i].wait()
        outs[i].start()
    loss_out[...] = loss_ref[...]
    for copy in outs:
        copy.wait()


def body(picture_vectors, sentence_vectors, slot_picture_number, score_multiplier, score_offset):
    vmem = pl.BlockSpec(memory_space=pltpu.VMEM)
    smem = pl.BlockSpec(memory_space=pltpu.SMEM)
    anywhere = pl.BlockSpec(memory_space=pl.ANY)
    parts = pl.pallas_call(
        kernel,
        out_shape=(
            jax.ShapeDtypeStruct((1, ROWS), F32),
            jax.ShapeDtypeStruct((ROWS, D), BF16),
            jax.ShapeDtypeStruct((16 * SLOT, D), BF16),
        ),
        in_specs=[smem, smem, vmem, vmem, anywhere],
        out_specs=(vmem, vmem, anywhere),
        scratch_shapes=[
            pltpu.VMEM((4, 512, D), BF16),
            pltpu.VMEM((4, 4, SLOT), jnp.int32),
            pltpu.VMEM((12 * ROWS, D), BF16),
            pltpu.VMEM((8 * ROWS, D), BF16),
            pltpu.VMEM((2, ROWS, D), BF16),
            pltpu.VMEM((2, ROWS, D), BF16),
            pltpu.VMEM((2, ROWS, D), BF16),
            pltpu.VMEM((2, ROWS, D), BF16),
            pltpu.VMEM((4, ROWS, 4 * SLOT), BF16),
            pltpu.VMEM((4, 4 * SLOT, ROWS), BF16),
            pltpu.VMEM((2 * ROWS, 8 * ROWS), BF16),
            pltpu.VMEM((ROWS, 8 * ROWS), BF16),
            pltpu.VMEM((ROWS, D), F32),
            pltpu.VMEM((2 * ROWS, D), F32),
            pltpu.VMEM((3, ROWS, D), BF16),
            pltpu.VMEM((4, ROWS, D), BF16),
            pltpu.VMEM((2, ROWS, D), BF16),
            pltpu.VMEM((2, ROWS, D), BF16),
            pltpu.VMEM((2, ROWS, 128), F32),
            pltpu.VMEM((2, ROWS, 128), F32),
            pltpu.SemaphoreType.DMA((N_COPY,)),
            pltpu.SemaphoreType.DMA((N_COPY,)),
            pltpu.SemaphoreType.DMA((16,)),
        ],
        compiler_params=pltpu.CompilerParams(
            collective_id=0, has_side_effects=True, vmem_limit_bytes=56 * 1024 * 1024
        ),
        cost_estimate=pl.CostEstimate(
            flops=13_000_000_000, bytes_accessed=12_000_000, transcendentals=4_000_000
        ),
        name="pooled_sigmoid_loss",
    )(
        score_multiplier.reshape(1),
        score_offset.reshape(1),
        slot_picture_number.reshape(4, 4, SLOT),
        picture_vectors,
        sentence_vectors,
    )
    loss, grad_images, grad_captions = pl.pallas_call(
        hand_over,
        out_shape=tuple(jax.ShapeDtypeStruct(p.shape, p.dtype) for p in parts),
        in_specs=[vmem, anywhere, anywhere],
        out_specs=(vmem, anywhere, anywhere),
        scratch_shapes=[
            pltpu.VMEM((9, ROWS, D), BF16),
            pltpu.SemaphoreType.DMA((9,)),
            pltpu.SemaphoreType.DMA((9,)),
        ],
        compiler_params=pltpu.CompilerParams(vmem_limit_bytes=60 * 1024 * 1024),
        name="hand_over",
    )(*parts)
    return loss.reshape(ROWS), grad_images, grad_captions


def solution(mesh):
    return jax.shard_map(
        body,
        mesh=mesh,
        in_specs=(
            P(("blk", "shard"), None),
            P(("blk", "shard"), None),
            P(("blk", "shard")),
            P(),
            P(),
        ),
        out_specs=(P(("blk", "shard")), P(("blk", "shard"), None), P(("blk", "shard"), None)),
        check_vma=False,
    )
```

```python
import jax
import jax.numpy as jnp
from jax import lax
from jax.experimental import pallas as pl
from jax.experimental.pallas import tpu as pltpu
from jax.sharding import PartitionSpec as P

EPS = 1e-06
D = 1152
ROWS = 256
SLOT = 128
NB = 16
TOTAL = NB * ROWS
F32 = jnp.float32
BF16 = jnp.bfloat16
WIDTHS_IN = (384, 384, 256, 128)
WIDTHS_OUT = (128, 256, 256, 256, 256)
N_COPY = 112


def spans(widths):
    starts = [sum(widths[:i]) for i in range(len(widths))]
    return [slice(s, s + n) for s, n in zip(starts, widths)]


IN, OUT = spans(WIDTHS_IN), spans(WIDTHS_OUT)


class Copy:
    def __init__(self, copy, when):
        self.copy, self.when = copy, when

    def act(self, step):
        if self.when is None:
            step()
        else:
            pl.when(self.when)(step)

    def wait_recv(self):
        self.act(self.copy.wait_recv)

    def wait_send(self):
        self.act(self.copy.wait_send)


def signed(scores, diagonal):
    return scores if diagonal is None else jnp.where(diagonal, -scores, scores)


def pair_gradient(scores, diagonal):
    sig = 1.0 / (1.0 + jnp.exp(-signed(scores, diagonal)))
    return signed(sig, diagonal)


def pair_terms(scores, diagonal):
    u = signed(scores, diagonal)
    e = jnp.exp(-jnp.abs(u))
    d = 1.0 + e
    r = 1.0 / d
    return signed(jnp.where(u >= 0, r, e * r), diagonal), jnp.maximum(u, 0.0), d


def kernel(
    mult_ref,
    off_ref,
    ids_ref,
    img_ref,
    cap_ref,
    loss_ref,
    gimg_ref,
    gcap_ref,
    xr,
    idr,
    imgs,
    txts,
    psib,
    prsib,
    psend,
    prec,
    hot,
    hot_t,
    g2,
    own2,
    lsum,
    lprod,
    tsum,
    tgrad,
    tswap,
    sc,
    gsend,
    grecv,
    lsend,
    lrecv,
    send_sem,
    recv_sem,
    local_sem,
):
    g = lax.axis_index("blk")
    h = lax.axis_index("shard")
    zh, y = lax.div(g, 4), lax.rem(g, 4)
    x, w = lax.div(h, 4), lax.rem(h, 4)
    zb = lax.rem(zh, 2)
    zl, b = lax.div(w, 2), lax.rem(w, 2)
    on = zb == b
    off = zb != b

    def ring(value, step):
        return lax.rem(value + step, 4)

    def at_x(step):
        return (g, ring(x, step) * 4 + w)

    def at_y(step):
        return (zh * 4 + ring(y, step), h)

    core = (g, x * 4 + zl * 2 + 1 - b)
    flipped = x * 4 + zl * 2 + 1 - b
    up = (jnp.where(on, ring(zh, 2), ring(zh, 1)) * 4 + y, jnp.where(on, h, flipped))
    down = (ring(zh, 3) * 4 + y, flipped)

    def home(step):
        to = 1 - zl if step else zl
        z = jnp.where(on, zh, ring(zh, jnp.where(to == 0, 1, 3)))
        return (z * 4 + y, x * 4 + to * 2 + jnp.where(on, b, 1 - b))

    def source(step):
        z = jnp.where(on, zh, ring(zh, jnp.where(zl == 0, 3, 1)))
        return (z * 4 + y, x * 4 + (1 - zl if step else zl) * 2 + jnp.where(on, b, 1 - b))

    def text_z(core_bit):
        return jnp.where(zb == core_bit, zh, ring(zh, jnp.where(zl == 0, 3, 1)))

    made = []
    local = []

    def send(src, dst, device, when=None, start=True):
        k = len(made)
        copy = pltpu.make_async_remote_copy(
            src_ref=src,
            dst_ref=dst,
            send_sem=send_sem.at[k],
            recv_sem=recv_sem.at[k],
            device_id=device,
            device_id_type=pl.DeviceIdType.MESH,
        )
        made.append(Copy(copy, when))
        if start:
            made[-1].act(copy.start)
        return made[-1]

    def move(src, dst):
        copy = pltpu.make_async_copy(src, dst, local_sem.at[len(local)])
        copy.start()
        local.append(copy)
        return copy

    def rows(block, first=0, count=ROWS):
        return pl.ds(pl.multiple_of(block * ROWS + first, 128), count)

    def piece(owner):
        return pl.ds(pl.multiple_of(owner * 512, 512), 512)

    barrier = pltpu.get_barrier_semaphore()

    def greet(device):
        pl.semaphore_signal(barrier, inc=1, device_id=device, device_id_type=pl.DeviceIdType.MESH)

    partners = [at_x(s) for s in (1, 2, 3)] + [at_y(s) for s in (1, 3)]
    partners += [core, up, home(1), source(1)]
    for device in partners:
        greet(device)

    @pl.when(off)
    def _():
        for device in (down, home(0), source(0)):
            greet(device)

    pl.semaphore_wait(barrier, len(partners) + jnp.where(on, 0, 3))

    id_copies = [send(ids_ref.at[ring(x, s)], idr.at[x], at_x(s)) for s in (2, 1, 3)]
    id_own = move(ids_ref.at[x], idr.at[x])
    x_copies, x_own = [], []
    for span in IN:
        x_copies.append(
            [
                send(cap_ref.at[piece(ring(x, s)), span], xr.at[x, :, span], at_x(s))
                for s in (2, 1, 3)
            ]
        )
        x_own.append(move(cap_ref.at[piece(x), span], xr.at[x, :, span]))

    pics = img_ref[...].astype(F32)
    pic_norm = jnp.sqrt(jnp.sum(pics * pics, axis=-1, keepdims=True) + EPS)
    imgs[rows(y), :] = (pics / pic_norm).astype(BF16)
    first = jnp.where(on, 0, 4)
    z_near = jnp.where(on, zh, ring(zh, 3))
    z_far = jnp.where(on, ring(zh, 2), ring(zh, 1))

    def round_y(buffer, slot, start=True):
        src = buffer.at[rows(slot(y))]
        return [send(src, src, at_y(s), start=start) for s in (1, 3)]

    def pass_y(buffer, slot, copies, step):
        copies[0 if step == 3 else 1].wait_recv()
        src = buffer.at[rows(slot(ring(y, step)), 0 if step == 3 else 128, 128)]
        return send(src, src, at_y(4 - step))

    def near_slot(k):
        return first + k

    def far_slot(k):
        return first + 4 + k

    def text_slot(k):
        return k * 2 + b

    src = imgs.at[rows(y)]
    up_copy = send(src, imgs.at[rows(4 + y)], up)
    down_copy = send(src, imgs.at[rows(8 + y)], down, when=off)
    near = round_y(imgs, near_slot, start=False)
    far = round_y(imgs, far_slot, start=False)

    @pl.when(on)
    def _():
        for copy in near:
            copy.copy.start()

    id_own.wait()
    for copy in id_copies:
        copy.wait_recv()
    image_rows = lax.broadcasted_iota(jnp.int32, (ROWS, SLOT), 0)
    for o in range(4):
        for s in range(4):
            table = (idr[s, o : o + 1, :] == image_rows).astype(F32)
            hot[o, :, s * SLOT : (s + 1) * SLOT] = table.astype(BF16)
            table = (ids_ref[s, o : o + 1, :] == image_rows).astype(F32)
            hot_t[s * 4 + o] = table.T.astype(BF16)

    up_copy.wait_recv()

    @pl.when(on)
    def _():
        for copy in far:
            copy.copy.start()

    @pl.when(off)
    def _():
        for copy in near:
            copy.copy.start()

    down_copy.wait_recv()

    @pl.when(off)
    def _():
        for copy in far:
            copy.copy.start()

    own2[:ROWS, :] = imgs[rows(near_slot(y)), :]
    own2[ROWS:, :] = imgs[rows(far_slot(y)), :]

    p_copies = []

    def pooled(owner, span):
        block = pl.ds(pl.multiple_of(owner * SLOT, SLOT), SLOT)
        stack = jnp.concatenate([xr[s, block, span] for s in range(4)], axis=0)
        return jnp.dot(hot[owner], stack, preferred_element_type=F32)

    def pool(j):
        span = IN[j]
        x_own[j].wait()
        for copy in x_copies[j]:
            copy.wait_recv()
        for t in range(2):
            psib[t, :, span] = pooled(t * 2 + 1 - b, span).astype(BF16)
        sib = send(psib.at[:, :, span], prsib.at[:, :, span], core)
        sums = [pooled(t * 2 + b, span) for t in range(2)]
        sib.wait_recv()
        for t in range(2):
            psend[t, :, span] = (sums[t] + prsib[t, :, span].astype(F32)).astype(BF16)
        p_copies.append(
            [
                send(psend.at[1 - zl, :, span], prec.at[1, :, span], home(1)),
                send(psend.at[zl, :, span], prec.at[0, :, span], home(0), when=off),
            ]
        )

        @pl.when(on)
        def _():
            prec[0, :, span] = psend[zl, :, span]

    pool(0)
    halves = [pass_y(imgs, near_slot, near, step) for step in (3, 1)]
    pool(1)
    halves += [pass_y(imgs, far_slot, far, step) for step in (3, 1)]
    for j in range(2, len(IN)):
        pool(j)

    square = jnp.zeros((ROWS, 1), F32)
    for j, span in enumerate(IN):
        for copy in p_copies[j]:
            copy.wait_recv()
        total = prec[0, :, span].astype(F32) + prec[1, :, span].astype(F32)
        tsum[:, span] = total
        square += jnp.sum(total * total, axis=-1, keepdims=True)
    text_scale = lax.rsqrt(square + EPS)
    unit = tsum[...] * text_scale
    tsum[...] = unit
    txts[rows(text_slot(y)), :] = unit.astype(BF16)
    src = txts.at[rows(text_slot(y))]
    t_swaps = [send(src, src, core)]
    t_copies = round_y(txts, text_slot)

    mult, offset = mult_ref[0], off_ref[0]
    gap = lax.broadcasted_iota(jnp.int32, (ROWS, ROWS), 0) - lax.broadcasted_iota(
        jnp.int32, (ROWS, ROWS), 1
    )
    nt = (((1,), (1,)), ((), ()))
    def diagonal(same):
        return gap == jnp.where(same, 0, 2 * ROWS)

    for copy in halves:
        copy.wait_recv()
    t_swaps[0].wait_recv()
    both = pl.ds(pl.multiple_of(y * 2 * ROWS, 128), 2 * ROWS)
    for step in (0, 3, 1, 2):
        for far_group, image_z in ((0, z_near), (1, z_far)):
            slot = far_group * 4 + ring(y, step)
            scores = lax.dot_general(
                txts[both, :], imgs[rows(first + slot), :], nt, preferred_element_type=F32
            )
            for t in range(2):
                block = slice(t * ROWS, (t + 1) * ROWS)
                mask = None if step else diagonal(image_z == text_z(t))
                grad = pair_gradient(mult * scores[block] + offset, mask)
                g2[block, rows(slot)] = grad.astype(BF16)
    parts = (slice(0, 512), slice(512, 1024), slice(1024, D))
    g_swaps = []
    for span in parts:
        tgrad[:, span] = mult * jnp.dot(
            g2[...],
            imgs[pl.ds(pl.multiple_of(first * ROWS, 128), 8 * ROWS), span],
            preferred_element_type=F32,
        )
        tswap[0, :, span] = tgrad[rows(1 - b), span].astype(BF16)
        g_swaps.append(send(tswap.at[0, :, span], tswap.at[1, :, span], core))

    along = jnp.zeros((ROWS, 1), F32)
    for copy, span in zip(g_swaps, parts):
        copy.wait_recv()
        total = tgrad[rows(b), span] + tswap[1, :, span].astype(F32)
        tgrad[rows(b), span] = total
        along += jnp.sum(tsum[:, span] * total, axis=-1, keepdims=True)
    s_copies = []
    for span in OUT:
        tswap[2, :, span] = (
            (tgrad[rows(b), span] - tsum[:, span] * along) * text_scale
        ).astype(BF16)
        src = tswap.at[2, :, span]
        s_copies.append(
            [
                send(src, sc.at[x, zb * 2 + zl, :, span], source(1)),
                send(src, sc.at[x, zb * 2 + zl, :, span], source(0), when=off),
            ]
        )

        @pl.when(on)
        def _():
            sc[x, zb * 2 + zl, :, span] = tswap[2, :, span]

    x_near = {}
    x_far = {}
    handed = {j: [] for j in range(len(OUT))}
    out_own = []

    def held(step, j, owner=None):
        if owner is None:
            return sc.at[ring(x, step), pl.ds(b * 2, 2), :, OUT[j]]
        return sc.at[ring(x, step), b * 2 + owner, :, OUT[j]]

    def hand(step, j):
        src = held(step, j)
        handed[j].append(send(src, src, core))

    def start_x(j):
        for copy in s_copies[j]:
            copy.wait_recv()
        src = held(0, j)
        x_near[j] = [send(src, src, at_x(s)) for s in (1, 3)]
        hand(0, j)

    def pass_x(j):
        x_far[j] = []
        for copy, step, owner in zip(x_near[j], (3, 1), (0, 1)):
            copy.wait_recv()
            src = held(step, j, owner)
            x_far[j].append(send(src, src, at_x(4 - step)))
            hand(step, j)

    def last_x(j):
        for copy in x_far[j]:
            copy.wait_recv()
        hand(2, j)

    def write(j):
        span = OUT[j]
        for copy in handed[j]:
            copy.wait_recv()
        for s in range(4):
            for o in range(4):
                xr[s, o * SLOT : (o + 1) * SLOT, span] = jnp.dot(
                    hot_t[s * 4 + o],
                    sc[s, o % 2 * 2 + o // 2, :, span],
                    preferred_element_type=F32,
                ).astype(BF16)
        out_own.append(move(xr.at[:, :, span], gcap_ref.at[:, :, span]))

    i_copies = []

    def image_pairs(step):
        column = ring(y, step) * 2 * ROWS
        texts = pl.ds(pl.multiple_of(column, 128), 2 * ROWS)
        scores = lax.dot_general(own2[...], txts[texts, :], nt, preferred_element_type=F32)
        for n, image_z in ((0, z_near), (1, z_far)):
            block = slice(n * ROWS, (n + 1) * ROWS)
            relu, prod = (lsum[block], lprod[block]) if step else (0.0, 1.0)
            for t in range(2):
                mask = None if step else diagonal(image_z == text_z(t))
                part = mult * scores[block, t * ROWS : (t + 1) * ROWS] + offset
                grad, positive, d = pair_terms(part, mask)
                relu += positive[:, :128] + positive[:, 128:]
                prod *= d[:, :128] * d[:, 128:]
                at = pl.ds(pl.multiple_of(column + t * ROWS, 128), ROWS)
                g2[block, at] = grad.astype(BF16)
            lsum[block] = relu
            lprod[block] = prod

    def image_grads(span):
        part = mult * jnp.dot(g2[...], txts[:, span], preferred_element_type=F32)
        for n, device, when in ((1, up, None), (0, down, off)):
            gsend[n, :, span] = part[n * ROWS : (n + 1) * ROWS].astype(BF16)
            i_copies.append(send(gsend.at[n, :, span], grecv.at[n, :, span], device, when))

    def image_losses():
        for n, device, when in ((1, up, None), (0, down, off)):
            block = slice(n * ROWS, (n + 1) * ROWS)
            lsend[n] = lsum[block] + jnp.log(lprod[block])
            i_copies.append(send(lsend.at[n], lrecv.at[n], device, when))

    start_x(0)
    t_halves = [pass_y(txts, text_slot, t_copies, step) for step in (3, 1)]
    for step in (3, 1):
        src = txts.at[rows(text_slot(ring(y, step)))]
        t_swaps.append(send(src, src, core))
    image_pairs(0)
    pass_x(0)
    t_swaps[1].wait_recv()
    image_pairs(3)
    start_x(1)
    t_swaps[2].wait_recv()
    image_pairs(1)
    for copy in t_halves:
        copy.wait_recv()
    src = txts.at[rows(text_slot(ring(y, 2)))]
    t_swaps.append(send(src, src, core))
    start_x(2)
    pass_x(1)
    t_swaps[3].wait_recv()
    image_pairs(2)
    image_grads(slice(0, 384))
    start_x(3)
    pass_x(2)
    last_x(0)
    image_grads(slice(384, 768))
    start_x(4)
    write(0)
    image_grads(slice(768, D))
    image_losses()
    pass_x(3)
    last_x(1)
    write(1)
    pass_x(4)
    last_x(2)
    write(2)
    last_x(3)
    write(3)
    last_x(4)
    write(4)

    @pl.when(on)
    def _():
        grecv[0] = gsend[0]
        lrecv[0] = lsend[0]

    for copy in i_copies:
        copy.wait_recv()

    losses = lrecv[0] + lrecv[1]
    loss_ref[...] = jnp.sum(losses.T, axis=0, keepdims=True) / TOTAL
    total = grecv[0].astype(F32) + grecv[1].astype(F32)
    pics = img_ref[...].astype(F32)
    pic_norm = jnp.sqrt(jnp.sum(pics * pics, axis=-1, keepdims=True) + EPS)
    unit = pics / pic_norm
    along = jnp.sum(unit * total, axis=-1, keepdims=True)
    gimg_ref[...] = ((total - unit * along) / pic_norm).astype(BF16)

    for copy in out_own:
        copy.wait()
    for copy in made:
        copy.wait_send()


def hand_over(loss_ref, gimg_ref, gcap_ref, loss_out, gimg_out, gcap_out, held, in_sem, out_sem):
    pieces = [(gcap_ref.at[i // 2], gcap_out.at[i // 2], i % 2 * ROWS) for i in range(8)]
    pieces.append((gimg_ref, gimg_out, 0))
    ins, outs = [], []
    for i, (src, dst, row) in enumerate(pieces):
        part = pl.ds(row, ROWS)
        ins.append(pltpu.make_async_copy(src.at[part], held.at[i], in_sem.at[i]))
        outs.append(pltpu.make_async_copy(held.at[i], dst.at[part], out_sem.at[i]))
        ins[i].start()
    for i in range(len(pieces)):
        ins[i].wait()
        outs[i].start()
    loss_out[...] = loss_ref[...]
    for copy in outs:
        copy.wait()


def body(picture_vectors, sentence_vectors, slot_picture_number, score_multiplier, score_offset):
    vmem = pl.BlockSpec(memory_space=pltpu.VMEM)
    smem = pl.BlockSpec(memory_space=pltpu.SMEM)
    anywhere = pl.BlockSpec(memory_space=pl.ANY)
    parts = pl.pallas_call(
        kernel,
        out_shape=(
            jax.ShapeDtypeStruct((1, ROWS), F32),
            jax.ShapeDtypeStruct((ROWS, D), BF16),
            jax.ShapeDtypeStruct((4, 4 * SLOT, D), BF16),
        ),
        in_specs=[smem, smem, vmem, vmem, anywhere],
        out_specs=(vmem, vmem, anywhere),
        scratch_shapes=[
            pltpu.VMEM((4, 512, D), BF16),
            pltpu.VMEM((4, 4, SLOT), jnp.int32),
            pltpu.VMEM((12 * ROWS, D), BF16),
            pltpu.VMEM((8 * ROWS, D), BF16),
            pltpu.VMEM((2, ROWS, D), BF16),
            pltpu.VMEM((2, ROWS, D), BF16),
            pltpu.VMEM((2, ROWS, D), BF16),
            pltpu.VMEM((2, ROWS, D), BF16),
            pltpu.VMEM((4, ROWS, 4 * SLOT), BF16),
            pltpu.VMEM((16, SLOT, ROWS), BF16),
            pltpu.VMEM((2 * ROWS, 8 * ROWS), BF16),
            pltpu.VMEM((2 * ROWS, D), BF16),
            pltpu.VMEM((2 * ROWS, 128), F32),
            pltpu.VMEM((2 * ROWS, 128), F32),
            pltpu.VMEM((ROWS, D), F32),
            pltpu.VMEM((2 * ROWS, D), F32),
            pltpu.VMEM((3, ROWS, D), BF16),
            pltpu.VMEM((4, 4, ROWS, D), BF16),
            pltpu.VMEM((2, ROWS, D), BF16),
            pltpu.VMEM((2, ROWS, D), BF16),
            pltpu.VMEM((2, ROWS, 128), F32),
            pltpu.VMEM((2, ROWS, 128), F32),
            pltpu.SemaphoreType.DMA((N_COPY,)),
            pltpu.SemaphoreType.DMA((N_COPY,)),
            pltpu.SemaphoreType.DMA((16,)),
        ],
        compiler_params=pltpu.CompilerParams(
            collective_id=0, has_side_effects=True, vmem_limit_bytes=56 * 1024 * 1024
        ),
        cost_estimate=pl.CostEstimate(
            flops=13_000_000_000, bytes_accessed=12_000_000, transcendentals=4_000_000
        ),
        name="pooled_sigmoid_loss",
    )(
        score_multiplier.reshape(1),
        score_offset.reshape(1),
        slot_picture_number.reshape(4, 4, SLOT),
        picture_vectors,
        sentence_vectors,
    )
    loss, grad_images, grad_captions = pl.pallas_call(
        hand_over,
        out_shape=tuple(jax.ShapeDtypeStruct(p.shape, p.dtype) for p in parts),
        in_specs=[vmem, anywhere, anywhere],
        out_specs=(vmem, anywhere, anywhere),
        scratch_shapes=[
            pltpu.VMEM((9, ROWS, D), BF16),
            pltpu.SemaphoreType.DMA((9,)),
            pltpu.SemaphoreType.DMA((9,)),
        ],
        compiler_params=pltpu.CompilerParams(vmem_limit_bytes=60 * 1024 * 1024),
        name="hand_over",
    )(*parts)
    return loss.reshape(ROWS), grad_images, grad_captions.reshape(16 * SLOT, D)


def solution(mesh):
    return jax.shard_map(
        body,
        mesh=mesh,
        in_specs=(
            P(("blk", "shard"), None),
            P(("blk", "shard"), None),
            P(("blk", "shard")),
            P(),
            P(),
        ),
        out_specs=(P(("blk", "shard")), P(("blk", "shard"), None), P(("blk", "shard"), None)),
        check_vma=False,
    )
```

```python
import jax
import jax.numpy as jnp
from jax import lax
from jax.experimental import pallas as pl
from jax.experimental.pallas import tpu as pltpu
from jax.sharding import PartitionSpec as P

EPS = 1e-06
D = 1152
ROWS = 256
SLOT = 128
NB = 16
TOTAL = NB * ROWS
F32 = jnp.float32
BF16 = jnp.bfloat16
WIDTHS_IN = (384, 384, 256, 128)
WIDTHS_OUT = (128, 256, 256, 256, 256)
N_COPY = 112


def spans(widths):
    starts = [sum(widths[:i]) for i in range(len(widths))]
    return [slice(s, s + n) for s, n in zip(starts, widths)]


IN, OUT = spans(WIDTHS_IN), spans(WIDTHS_OUT)


class Copy:
    def __init__(self, copy, when):
        self.copy, self.when = copy, when

    def act(self, step):
        if self.when is None:
            step()
        else:
            pl.when(self.when)(step)

    def wait_recv(self):
        self.act(self.copy.wait_recv)

    def wait_send(self):
        self.act(self.copy.wait_send)


def signed(scores, diagonal):
    return scores if diagonal is None else jnp.where(diagonal, -scores, scores)


def pair_gradient(scores, diagonal):
    sig = 1.0 / (1.0 + jnp.exp(-signed(scores, diagonal)))
    return signed(sig, diagonal)


def pair_terms(scores, diagonal):
    u = signed(scores, diagonal)
    e = jnp.exp(-jnp.abs(u))
    d = 1.0 + e
    r = 1.0 / d
    return signed(jnp.where(u >= 0, r, e * r), diagonal), jnp.maximum(u, 0.0), d


def kernel(
    mult_ref,
    off_ref,
    ids_ref,
    img_ref,
    cap_ref,
    loss_ref,
    gimg_ref,
    gcap_ref,
    xr,
    idr,
    imgs,
    txts,
    psib,
    prsib,
    psend,
    prec,
    hot,
    hot_t,
    g2,
    own2,
    iunit,
    along_sum,
    along_got,
    lsum,
    lprod,
    tsum,
    tgrad,
    tswap,
    sc,
    gsend,
    grecv,
    lsend,
    lrecv,
    send_sem,
    recv_sem,
    local_sem,
):
    g = lax.axis_index("blk")
    h = lax.axis_index("shard")
    zh, y = lax.div(g, 4), lax.rem(g, 4)
    x, w = lax.div(h, 4), lax.rem(h, 4)
    zb = lax.rem(zh, 2)
    zl, b = lax.div(w, 2), lax.rem(w, 2)
    on = zb == b
    off = zb != b

    def ring(value, step):
        return lax.rem(value + step, 4)

    def at_x(step):
        return (g, ring(x, step) * 4 + w)

    def at_y(step):
        return (zh * 4 + ring(y, step), h)

    core = (g, x * 4 + zl * 2 + 1 - b)
    flipped = x * 4 + zl * 2 + 1 - b
    up = (jnp.where(on, ring(zh, 2), ring(zh, 1)) * 4 + y, jnp.where(on, h, flipped))
    down = (ring(zh, 3) * 4 + y, flipped)

    def home(step):
        to = 1 - zl if step else zl
        z = jnp.where(on, zh, ring(zh, jnp.where(to == 0, 1, 3)))
        return (z * 4 + y, x * 4 + to * 2 + jnp.where(on, b, 1 - b))

    def source(step):
        z = jnp.where(on, zh, ring(zh, jnp.where(zl == 0, 3, 1)))
        return (z * 4 + y, x * 4 + (1 - zl if step else zl) * 2 + jnp.where(on, b, 1 - b))

    def text_z(core_bit):
        return jnp.where(zb == core_bit, zh, ring(zh, jnp.where(zl == 0, 3, 1)))

    made = []
    local = []

    def send(src, dst, device, when=None, start=True):
        k = len(made)
        copy = pltpu.make_async_remote_copy(
            src_ref=src,
            dst_ref=dst,
            send_sem=send_sem.at[k],
            recv_sem=recv_sem.at[k],
            device_id=device,
            device_id_type=pl.DeviceIdType.MESH,
        )
        made.append(Copy(copy, when))
        if start:
            made[-1].act(copy.start)
        return made[-1]

    def move(src, dst):
        copy = pltpu.make_async_copy(src, dst, local_sem.at[len(local)])
        copy.start()
        local.append(copy)
        return copy

    def rows(block, first=0, count=ROWS):
        return pl.ds(pl.multiple_of(block * ROWS + first, 128), count)

    def piece(owner):
        return pl.ds(pl.multiple_of(owner * 512, 512), 512)

    barrier = pltpu.get_barrier_semaphore()

    def greet(device):
        pl.semaphore_signal(barrier, inc=1, device_id=device, device_id_type=pl.DeviceIdType.MESH)

    partners = [at_x(s) for s in (1, 2, 3)] + [at_y(s) for s in (1, 3)]
    partners += [core, up, home(1), source(1)]
    for device in partners:
        greet(device)

    @pl.when(off)
    def _():
        for device in (down, home(0), source(0)):
            greet(device)

    pl.semaphore_wait(barrier, len(partners) + jnp.where(on, 0, 3))

    id_copies = [send(ids_ref.at[ring(x, s)], idr.at[x], at_x(s)) for s in (2, 1, 3)]
    id_own = move(ids_ref.at[x], idr.at[x])
    x_copies, x_own = [], []
    for span in IN:
        x_copies.append(
            [
                send(cap_ref.at[piece(ring(x, s)), span], xr.at[x, :, span], at_x(s))
                for s in (2, 1, 3)
            ]
        )
        x_own.append(move(cap_ref.at[piece(x), span], xr.at[x, :, span]))

    pics = img_ref[...].astype(F32)
    pic_norm = jnp.sqrt(jnp.sum(pics * pics, axis=-1, keepdims=True) + EPS)
    pic_scale = 1.0 / pic_norm
    iunit[...] = pics * pic_scale
    imgs[rows(y), :] = iunit[...].astype(BF16)
    first = jnp.where(on, 0, 4)
    z_near = jnp.where(on, zh, ring(zh, 3))
    z_far = jnp.where(on, ring(zh, 2), ring(zh, 1))

    def round_y(buffer, slot, start=True):
        src = buffer.at[rows(slot(y))]
        return [send(src, src, at_y(s), start=start) for s in (1, 3)]

    def pass_y(buffer, slot, copies, step):
        copies[0 if step == 3 else 1].wait_recv()
        src = buffer.at[rows(slot(ring(y, step)), 0 if step == 3 else 128, 128)]
        return send(src, src, at_y(4 - step))

    def near_slot(k):
        return first + k

    def far_slot(k):
        return first + 4 + k

    def text_slot(k):
        return k * 2 + b

    src = imgs.at[rows(y)]
    up_copy = send(src, imgs.at[rows(4 + y)], up)
    down_copy = send(src, imgs.at[rows(8 + y)], down, when=off)
    near = round_y(imgs, near_slot, start=False)
    far = round_y(imgs, far_slot, start=False)

    @pl.when(on)
    def _():
        for copy in near:
            copy.copy.start()

    id_own.wait()
    for copy in id_copies:
        copy.wait_recv()
    image_rows = lax.broadcasted_iota(jnp.int32, (ROWS, SLOT), 0)
    for o in range(4):
        for s in range(4):
            table = (idr[s, o : o + 1, :] == image_rows).astype(F32)
            hot[o, :, s * SLOT : (s + 1) * SLOT] = table.astype(BF16)
            table = (ids_ref[s, o : o + 1, :] == image_rows).astype(F32)
            hot_t[s * 4 + o] = table.T.astype(BF16)

    up_copy.wait_recv()

    @pl.when(on)
    def _():
        for copy in far:
            copy.copy.start()

    @pl.when(off)
    def _():
        for copy in near:
            copy.copy.start()

    down_copy.wait_recv()

    @pl.when(off)
    def _():
        for copy in far:
            copy.copy.start()

    own2[:ROWS, :] = imgs[rows(near_slot(y)), :]
    own2[ROWS:, :] = imgs[rows(far_slot(y)), :]

    p_copies = []

    def pooled(owner, span):
        block = pl.ds(pl.multiple_of(owner * SLOT, SLOT), SLOT)
        stack = jnp.concatenate([xr[s, block, span] for s in range(4)], axis=0)
        return jnp.dot(hot[owner], stack, preferred_element_type=F32)

    def pool(j):
        span = IN[j]
        x_own[j].wait()
        for copy in x_copies[j]:
            copy.wait_recv()
        for t in range(2):
            psib[t, :, span] = pooled(t * 2 + 1 - b, span).astype(BF16)
        sib = send(psib.at[:, :, span], prsib.at[:, :, span], core)
        sums = [pooled(t * 2 + b, span) for t in range(2)]
        sib.wait_recv()
        for t in range(2):
            psend[t, :, span] = (sums[t] + prsib[t, :, span].astype(F32)).astype(BF16)
        p_copies.append(
            [
                send(psend.at[1 - zl, :, span], prec.at[1, :, span], home(1)),
                send(psend.at[zl, :, span], prec.at[0, :, span], home(0), when=off),
            ]
        )

        @pl.when(on)
        def _():
            prec[0, :, span] = psend[zl, :, span]

    pool(0)
    halves = [pass_y(imgs, near_slot, near, step) for step in (3, 1)]
    pool(1)
    halves += [pass_y(imgs, far_slot, far, step) for step in (3, 1)]
    for j in range(2, len(IN)):
        pool(j)

    square = jnp.zeros((ROWS, 1), F32)
    for j, span in enumerate(IN):
        for copy in p_copies[j]:
            copy.wait_recv()
        total = prec[0, :, span].astype(F32) + prec[1, :, span].astype(F32)
        tsum[:, span] = total
        square += jnp.sum(total * total, axis=-1, keepdims=True)
    text_scale = lax.rsqrt(square + EPS)
    unit = tsum[...] * text_scale
    tsum[...] = unit
    txts[rows(text_slot(y)), :] = unit.astype(BF16)
    src = txts.at[rows(text_slot(y))]
    t_swaps = [send(src, src, core)]
    t_copies = round_y(txts, text_slot)

    mult, offset = mult_ref[0], off_ref[0]
    gap = lax.broadcasted_iota(jnp.int32, (ROWS, ROWS), 0) - lax.broadcasted_iota(
        jnp.int32, (ROWS, ROWS), 1
    )
    nt = (((1,), (1,)), ((), ()))
    def diagonal(same):
        return gap == jnp.where(same, 0, 2 * ROWS)

    for copy in halves:
        copy.wait_recv()
    t_swaps[0].wait_recv()
    both = pl.ds(pl.multiple_of(y * 2 * ROWS, 128), 2 * ROWS)
    along_parts = [jnp.zeros((ROWS, 128), F32)] * 2
    for step in (0, 3, 1, 2):
        for far_group, image_z in ((0, z_near), (1, z_far)):
            slot = far_group * 4 + ring(y, step)
            scores = lax.dot_general(
                txts[both, :], imgs[rows(first + slot), :], nt, preferred_element_type=F32
            )
            for t in range(2):
                block = slice(t * ROWS, (t + 1) * ROWS)
                mask = None if step else diagonal(image_z == text_z(t))
                part = mult * scores[block]
                grad = pair_gradient(part + offset, mask).astype(BF16)
                g2[block, rows(slot)] = grad
                part = grad.astype(F32) * part
                along_parts[t] += part[:, :128] + part[:, 128:]
    for t in range(2):
        along_sum[t] = along_parts[t]
    along_swap = send(along_sum.at[1 - b], along_got, core)

    g_swaps, s_copies = [], []

    def text_grad(j):
        span = OUT[j]
        tgrad[:, span] = mult * jnp.dot(
            g2[...],
            imgs[pl.ds(pl.multiple_of(first * ROWS, 128), 8 * ROWS), span],
            preferred_element_type=F32,
        )
        tswap[0, :, span] = tgrad[rows(1 - b), span].astype(BF16)
        g_swaps.append(send(tswap.at[0, :, span], tswap.at[1, :, span], core))

    def scale(j):
        span = OUT[j]
        g_swaps[j].wait_recv()
        total = tgrad[rows(b), span] + tswap[1, :, span].astype(F32)
        tswap[2, :, span] = ((total - tsum[:, span] * along) * text_scale).astype(BF16)
        src = tswap.at[2, :, span]
        s_copies.append(
            [
                send(src, sc.at[x, zb * 2 + zl, :, span], source(1)),
                send(src, sc.at[x, zb * 2 + zl, :, span], source(0), when=off),
            ]
        )

        @pl.when(on)
        def _():
            sc[x, zb * 2 + zl, :, span] = tswap[2, :, span]

    text_grad(0)
    text_grad(1)
    along_swap.wait_recv()
    along = jnp.sum(along_sum[b] + along_got[...], axis=-1, keepdims=True)
    scale(0)
    text_grad(2)
    scale(1)
    text_grad(3)
    scale(2)
    text_grad(4)
    scale(3)
    scale(4)

    x_near = {}
    x_far = {}
    handed = {j: [] for j in range(len(OUT))}
    out_own = []

    def held(step, j, owner=None):
        if owner is None:
            return sc.at[ring(x, step), pl.ds(b * 2, 2), :, OUT[j]]
        return sc.at[ring(x, step), b * 2 + owner, :, OUT[j]]

    def hand(step, j):
        src = held(step, j)
        handed[j].append(send(src, src, core))

    def start_x(j):
        for copy in s_copies[j]:
            copy.wait_recv()
        src = held(0, j)
        x_near[j] = [send(src, src, at_x(s)) for s in (1, 3)]
        hand(0, j)

    def pass_x(j):
        x_far[j] = []
        for copy, step, owner in zip(x_near[j], (3, 1), (0, 1)):
            copy.wait_recv()
            src = held(step, j, owner)
            x_far[j].append(send(src, src, at_x(4 - step)))
            hand(step, j)

    def last_x(j):
        for copy in x_far[j]:
            copy.wait_recv()
        hand(2, j)

    def write(j):
        span = OUT[j]
        for copy in handed[j]:
            copy.wait_recv()
        for s in range(4):
            for o in range(4):
                xr[s, o * SLOT : (o + 1) * SLOT, span] = jnp.dot(
                    hot_t[s * 4 + o],
                    sc[s, o % 2 * 2 + o // 2, :, span],
                    preferred_element_type=F32,
                ).astype(BF16)
        out_own.append(move(xr.at[:, :, span], gcap_ref.at[:, :, span]))

    i_copies = []

    def image_pairs(step):
        column = ring(y, step) * 2 * ROWS
        texts = pl.ds(pl.multiple_of(column, 128), 2 * ROWS)
        scores = lax.dot_general(own2[...], txts[texts, :], nt, preferred_element_type=F32)
        for n, image_z in ((0, z_near), (1, z_far)):
            block = slice(n * ROWS, (n + 1) * ROWS)
            relu, prod = (lsum[block], lprod[block]) if step else (0.0, 1.0)
            for t in range(2):
                mask = None if step else diagonal(image_z == text_z(t))
                part = mult * scores[block, t * ROWS : (t + 1) * ROWS] + offset
                grad, positive, d = pair_terms(part, mask)
                relu += positive[:, :128] + positive[:, 128:]
                prod *= d[:, :128] * d[:, 128:]
                at = pl.ds(pl.multiple_of(column + t * ROWS, 128), ROWS)
                g2[block, at] = grad.astype(BF16)
            lsum[block] = relu
            lprod[block] = prod

    def image_grads(span):
        part = mult * jnp.dot(g2[...], txts[:, span], preferred_element_type=F32)
        for n, device, when in ((1, up, None), (0, down, off)):
            gsend[n, :, span] = part[n * ROWS : (n + 1) * ROWS].astype(BF16)
            i_copies.append(send(gsend.at[n, :, span], grecv.at[n, :, span], device, when))

    def image_losses():
        for n, device, when in ((1, up, None), (0, down, off)):
            block = slice(n * ROWS, (n + 1) * ROWS)
            lsend[n] = lsum[block] + jnp.log(lprod[block])
            i_copies.append(send(lsend.at[n], lrecv.at[n], device, when))

    start_x(0)
    t_halves = [pass_y(txts, text_slot, t_copies, step) for step in (3, 1)]
    for step in (3, 1):
        src = txts.at[rows(text_slot(ring(y, step)))]
        t_swaps.append(send(src, src, core))
    image_pairs(0)
    pass_x(0)
    t_swaps[1].wait_recv()
    image_pairs(3)
    start_x(1)
    t_swaps[2].wait_recv()
    image_pairs(1)
    for copy in t_halves:
        copy.wait_recv()
    src = txts.at[rows(text_slot(ring(y, 2)))]
    t_swaps.append(send(src, src, core))
    start_x(2)
    pass_x(1)
    t_swaps[3].wait_recv()
    image_pairs(2)
    image_grads(slice(0, 384))
    start_x(3)
    pass_x(2)
    last_x(0)
    image_grads(slice(384, 768))
    start_x(4)
    write(0)
    image_grads(slice(768, D))
    image_losses()
    pass_x(3)
    last_x(1)
    write(1)
    pass_x(4)
    last_x(2)
    write(2)
    last_x(3)
    write(3)
    last_x(4)
    write(4)

    @pl.when(on)
    def _():
        grecv[0] = gsend[0]
        lrecv[0] = lsend[0]

    for copy in i_copies:
        copy.wait_recv()

    losses = lrecv[0] + lrecv[1]
    loss_ref[...] = jnp.sum(losses.T, axis=0, keepdims=True) / TOTAL
    total = grecv[0].astype(F32) + grecv[1].astype(F32)
    unit = iunit[...]
    along = jnp.sum(unit * total, axis=-1, keepdims=True)
    gimg_ref[...] = ((total - unit * along) * pic_scale).astype(BF16)

    for copy in out_own:
        copy.wait()
    for copy in made:
        copy.wait_send()


def hand_over(loss_ref, gimg_ref, gcap_ref, loss_out, gimg_out, gcap_out, held, in_sem, out_sem):
    pieces = [(gcap_ref.at[i // 2], gcap_out.at[i // 2], i % 2 * ROWS) for i in range(8)]
    pieces.append((gimg_ref, gimg_out, 0))
    ins, outs = [], []
    for i, (src, dst, row) in enumerate(pieces):
        part = pl.ds(row, ROWS)
        ins.append(pltpu.make_async_copy(src.at[part], held.at[i], in_sem.at[i]))
        outs.append(pltpu.make_async_copy(held.at[i], dst.at[part], out_sem.at[i]))
        ins[i].start()
    for i in range(len(pieces)):
        ins[i].wait()
        outs[i].start()
    loss_out[...] = loss_ref[...]
    for copy in outs:
        copy.wait()


def body(picture_vectors, sentence_vectors, slot_picture_number, score_multiplier, score_offset):
    vmem = pl.BlockSpec(memory_space=pltpu.VMEM)
    smem = pl.BlockSpec(memory_space=pltpu.SMEM)
    anywhere = pl.BlockSpec(memory_space=pl.ANY)
    parts = pl.pallas_call(
        kernel,
        out_shape=(
            jax.ShapeDtypeStruct((1, ROWS), F32),
            jax.ShapeDtypeStruct((ROWS, D), BF16),
            jax.ShapeDtypeStruct((4, 4 * SLOT, D), BF16),
        ),
        in_specs=[smem, smem, vmem, vmem, anywhere],
        out_specs=(vmem, vmem, anywhere),
        scratch_shapes=[
            pltpu.VMEM((4, 512, D), BF16),
            pltpu.VMEM((4, 4, SLOT), jnp.int32),
            pltpu.VMEM((12 * ROWS, D), BF16),
            pltpu.VMEM((8 * ROWS, D), BF16),
            pltpu.VMEM((2, ROWS, D), BF16),
            pltpu.VMEM((2, ROWS, D), BF16),
            pltpu.VMEM((2, ROWS, D), BF16),
            pltpu.VMEM((2, ROWS, D), BF16),
            pltpu.VMEM((4, ROWS, 4 * SLOT), BF16),
            pltpu.VMEM((16, SLOT, ROWS), BF16),
            pltpu.VMEM((2 * ROWS, 8 * ROWS), BF16),
            pltpu.VMEM((2 * ROWS, D), BF16),
            pltpu.VMEM((ROWS, D), F32),
            pltpu.VMEM((2, ROWS, 128), F32),
            pltpu.VMEM((ROWS, 128), F32),
            pltpu.VMEM((2 * ROWS, 128), F32),
            pltpu.VMEM((2 * ROWS, 128), F32),
            pltpu.VMEM((ROWS, D), F32),
            pltpu.VMEM((2 * ROWS, D), F32),
            pltpu.VMEM((3, ROWS, D), BF16),
            pltpu.VMEM((4, 4, ROWS, D), BF16),
            pltpu.VMEM((2, ROWS, D), BF16),
            pltpu.VMEM((2, ROWS, D), BF16),
            pltpu.VMEM((2, ROWS, 128), F32),
            pltpu.VMEM((2, ROWS, 128), F32),
            pltpu.SemaphoreType.DMA((N_COPY,)),
            pltpu.SemaphoreType.DMA((N_COPY,)),
            pltpu.SemaphoreType.DMA((16,)),
        ],
        compiler_params=pltpu.CompilerParams(
            collective_id=0, has_side_effects=True, vmem_limit_bytes=56 * 1024 * 1024
        ),
        cost_estimate=pl.CostEstimate(
            flops=13_000_000_000, bytes_accessed=12_000_000, transcendentals=4_000_000
        ),
        name="pooled_sigmoid_loss",
    )(
        score_multiplier.reshape(1),
        score_offset.reshape(1),
        slot_picture_number.reshape(4, 4, SLOT),
        picture_vectors,
        sentence_vectors,
    )
    loss, grad_images, grad_captions = pl.pallas_call(
        hand_over,
        out_shape=tuple(jax.ShapeDtypeStruct(p.shape, p.dtype) for p in parts),
        in_specs=[vmem, anywhere, anywhere],
        out_specs=(vmem, anywhere, anywhere),
        scratch_shapes=[
            pltpu.VMEM((9, ROWS, D), BF16),
            pltpu.SemaphoreType.DMA((9,)),
            pltpu.SemaphoreType.DMA((9,)),
        ],
        compiler_params=pltpu.CompilerParams(vmem_limit_bytes=60 * 1024 * 1024),
        name="hand_over",
    )(*parts)
    return loss.reshape(ROWS), grad_images, grad_captions.reshape(16 * SLOT, D)


def solution(mesh):
    return jax.shard_map(
        body,
        mesh=mesh,
        in_specs=(
            P(("blk", "shard"), None),
            P(("blk", "shard"), None),
            P(("blk", "shard")),
            P(),
            P(),
        ),
        out_specs=(P(("blk", "shard")), P(("blk", "shard"), None), P(("blk", "shard"), None)),
        check_vma=False,
    )
```
